32 devices in a mesh: req: 8 (over z, y), mlp: 4 (over x, core).
Axes of the slice: x: 2, y: 2, z: 4, core: 2. Of those that a mesh axis runs over, the one named last changes fastest.
Arguments:
- queries: bfloat16 [8, 2, 16, 2, 1536], P('req', None, 'mlp'), may hold values from -64 to 64
- new_kv: bfloat16 [8, 2, 16, 2, 256], P('req', None, 'mlp'), may hold values from -9 to 9
- residual: bfloat16 [8, 2, 16, 2, 1536], P('req', None, 'mlp'), may hold values from -3 to 3
- prompt_kv: bfloat16 [8, 1024, 256], P('req'), may hold values from -9 to 9
- tail_kv: bfloat16 [8, 16, 64, 256], P('req', 'mlp'), may hold values from -9 to 9
- page_pool: bfloat16 [256, 160, 256], P(('req', 'mlp')), may hold values from -9 to 9
- page_holder: int32 [32, 8], P(('req', 'mlp')), may hold values from 0 to 7, as said below
- serve_slot: int32 [32, 8], P(('req', 'mlp')), may hold values from 0 to 7
- prompt_len: int32 [8, 2], P('req'), may hold values from 512 to 32768
- tail_len: int32 [8, 2, 16], P('req', None, 'mlp'), may hold values from 1 to 62, 496 in all within a row
- w_out: bfloat16 [1536, 1536], P('mlp'), may hold values from -0.15625 to 0.15625
- norm_mlp: float32 [1536], replicated, may hold values from 0.25 to 1.75
- w_gate: bfloat16 [1536, 4608], P(None, 'mlp'), may hold values from -0.15625 to 0.15625
- w_up: bfloat16 [1536, 4608], P(None, 'mlp'), may hold values from -0.15625 to 0.15625
- w_down: bfloat16 [4608, 1536], P('mlp'), may hold values from -0.09375 to 0.09375
- norm_final: float32 [1536], replicated, may hold values from 0.25 to 1.75
- w_score: float32 [1536], replicated, may hold values from -0.15625 to 0.15625
Outputs:
- scores: float32 [8, 2, 16, 2], P('req', None, 'mlp')
- hidden_out: bfloat16 [8, 2, 16, 2, 1536], P('req', None, 'mlp')
- tails_out: bfloat16 [8, 2, 16, 64, 256], P('req', None, 'mlp')
The draws below stay inside these ranges and needn't reach their ends.
Inputs may be any that keep to these rules, and one draw needn't show every extreme that they name: Each row of page_holder names every req index once.
All inputs are finite; a program needn't handle non-finite values. No bound on the sum of `tail_len` on one device may be relied on, other than what follows from the above.
Results may differ from the reference program's by a relative error of at most 0.015.
Values may be sent and summed in bfloat16 or wider, within the bound.
A program may use at most 64 MiB of HBM per device.

```python
import math
import jax
import jax.numpy as jnp
import numpy as np
from jax import lax

D = 1536
FF = 4608
H = 12
HD = 128
WIN = 1024
SAMPLES = 16
TAIL = 64
PAGE = 160
N_REQ = 8
N_MLP = 4


def draw_queries(key, part):
    shape = (N_REQ, 2, SAMPLES, 2, H * HD)
    base = jnp.clip(jax.random.normal(jax.random.fold_in(key, 11), shape, jnp.float32), -4.0, 4.0)
    return base.astype(jnp.bfloat16)


def draw_page_holder(key, part):
    keys = jax.random.split(jax.random.fold_in(key, 21), N_REQ * N_MLP)
    table = jax.vmap(lambda k: jax.random.permutation(k, N_REQ))(keys)
    return table.astype(jnp.int32)


def place_ends(array, own_key, least, top_value):
    longest = array.shape.index(max(array.shape))
    spots = []
    for shift in (0, 1):
        where = [jax.random.randint(jax.random.fold_in(own_key, axis), (), 0, length) for axis, length in enumerate(array.shape)]
        where[longest] = (where[longest] + shift) % array.shape[longest]
        spots.append(tuple(where))
    return array.at[spots[0]].set(least).at[spots[1]].set(top_value)


def steps_of(key, extent, pieces, low, top_value):
    def one(position, parts):
        draws = jax.random.uniform(jax.random.fold_in(jax.random.fold_in(key, 6), position), (parts,), jnp.float32, low / len(pieces), top_value / len(pieces))
        return jnp.repeat(jnp.exp(draws), extent[position] // parts).reshape((-1,) + (1,) * (len(extent) - position - 1))

    factor_of = one(*pieces[0])
    for cut in pieces[1:]:
        factor_of = factor_of * one(*cut)
    return factor_of


def split_up(count, total, bound, lean):
    weights = [(1 << 20) // math.isqrt(grade ** lean) + 1 for grade in range(2, count + 1)]
    spare, holding = total - bound - (count - 1), [1] * (count - 1)
    while spare > 0:
        candidates = [i for i in range(count - 1) if holding[i] < bound]
        pool, remaining = sum([weights[i] for i in candidates]), spare
        for i in candidates:
            extra = min(bound - holding[i], max(1, remaining * weights[i] // pool), spare)
            holding[i] = holding[i] + extra
            spare = spare - extra
    return np.array([bound] + holding)


def ragged(key, amount, total, most, slope):
    if amount == 2:
        one = jax.random.randint(key, (), max(1, total - most), min(most, total - 1) + 1)
        return jnp.stack([one, total - one])
    tallies = jnp.asarray(split_up(amount, total, most, slope), jnp.int32)
    twos = (amount - 1) // 2
    source_of, sink = tallies[1:1 + 2 * twos:2], tallies[2:2 + 2 * twos:2]
    slack = jnp.minimum(source_of - 1, most - sink)
    passed = jax.random.randint(jax.random.fold_in(key, 1), (twos,), 0, 1 << 20) % (slack + 1)
    tallies = tallies.at[1:1 + 2 * twos:2].set(source_of - passed).at[2:2 + 2 * twos:2].set(sink + passed)
    return tallies[jax.random.permutation(jax.random.fold_in(key, 2), amount)]


def noise(rng, dims, spread, reach, cuts=(), kind=jnp.bfloat16):
    entries = jax.random.normal(rng, dims, jnp.float32) * spread
    if len(cuts) > 0:
        entries = steps_of(rng, dims, cuts, -0.22, 0.18) * entries
    return jnp.clip(entries, min=-reach, max=reach).astype(kind)


def setup_inputs(seed: int = 0) -> dict:
    key_of = jax.random.split(jax.random.key(seed), 18)
    return {
        "queries": draw_queries(jax.random.fold_in(key_of[17], 71), 0),
        "new_kv": noise(key_of[1], (N_REQ, 2, SAMPLES, 2, 2 * HD), 1.5, 9.0, ((0, 8), (2, 4))),
        "residual": noise(key_of[2], (N_REQ, 2, SAMPLES, 2, D), 0.5, 3.0, ((0, 8), (2, 4))),
        "prompt_kv": noise(key_of[3], (N_REQ, WIN, 2 * HD), 1.5, 9.0, ((0, 8),)),
        "tail_kv": noise(key_of[4], (N_REQ, SAMPLES, TAIL, 2 * HD), 1.5, 9.0, ((0, 8), (1, 4))),
        "page_pool": noise(key_of[5], (N_REQ * N_MLP * N_REQ, PAGE, 2 * HD), 1.5, 9.0, ((0, 32),)),
        "page_holder": draw_page_holder(jax.random.fold_in(key_of[17], 71), 0),
        "serve_slot": place_ends(jax.random.randint(key_of[7], (N_REQ * N_MLP, N_REQ), 0, N_REQ), jax.random.fold_in(key_of[7], 1), 0, N_REQ - 1).astype(jnp.int32),
        "prompt_len": place_ends(jax.random.randint(key_of[8], (N_REQ, 2), WIN // 2, 32 * WIN + 1), jax.random.fold_in(key_of[8], 1), WIN // 2, 32 * WIN).astype(jnp.int32),
        "tail_len": jax.vmap(lambda own: ragged(own, SAMPLES, SAMPLES * (TAIL - 2) // 2, TAIL - 2, 2))(jax.random.split(key_of[9], N_REQ * 2)).reshape((N_REQ, 2, SAMPLES)).astype(jnp.int32),
        "w_out": noise(key_of[10], (H * HD, D), (H * HD) ** -0.5, 0.15625, ((0, 4),)),
        "norm_mlp": jnp.clip(1.0 + 0.15 * jax.random.normal(key_of[11], (D,), jnp.float32), 0.25, 1.75),
        "w_gate": noise(key_of[12], (D, FF), D ** -0.5, 0.15625, ((1, 4),)),
        "w_up": noise(key_of[13], (D, FF), D ** -0.5, 0.15625, ((1, 4),)),
        "w_down": noise(key_of[14], (FF, D), FF ** -0.5, 0.09375, ((0, 4),)),
        "norm_final": jnp.clip(1.0 + 0.15 * jax.random.normal(key_of[15], (D,), jnp.float32), 0.25, 1.75),
        "w_score": noise(key_of[16], (D,), D ** -0.5, 0.15625, (), jnp.float32),
    }


def attend(query, fresh, window, tails, plen, tlen):
    count = query.shape[0]
    size = window.shape[-1] // 2
    q = query.reshape(count, 2, -1, size).astype(jnp.float32)
    scale = 1.0 / jnp.sqrt(jnp.float32(size))
    wk = window[:, :size].astype(jnp.float32)
    wv = window[:, size:].astype(jnp.float32)
    tk = tails[..., :size].astype(jnp.float32)
    tv = tails[..., size:].astype(jnp.float32)
    nk = fresh[..., :size].astype(jnp.float32)
    nv = fresh[..., size:].astype(jnp.float32)
    s_win = jnp.einsum('sthd,kd->sthk', q, wk) * scale
    s_tail = jnp.einsum('sthd,sjd->sthj', q, tk) * scale
    s_new = jnp.einsum('sthd,sud->sthu', q, nk) * scale
    tpos = tlen[:, None] + jnp.arange(2, dtype=jnp.int32)[None, :]
    kw = jnp.arange(window.shape[0], dtype=jnp.int32)[None, None, None, :]
    ok_win = (kw >= window.shape[0] - plen) & (kw > tpos[:, :, None, None])
    kt = jnp.arange(tails.shape[1], dtype=jnp.int32)[None, None, None, :]
    ok_tail = kt < tlen[:, None, None, None]
    steps = jnp.arange(2, dtype=jnp.int32)
    ok_new = steps[None, None, None, :] <= steps[None, :, None, None]
    s_win = jnp.where(ok_win, s_win, -1e+30)
    s_tail = jnp.where(ok_tail, s_tail, -1e+30)
    s_new = jnp.where(ok_new, s_new, -1e+30)
    top = jnp.maximum(jnp.maximum(s_win.max(-1), s_tail.max(-1)), s_new.max(-1))[..., None]
    e_win = jnp.where(ok_win, jnp.exp(s_win - top), 0.0)
    e_tail = jnp.where(ok_tail, jnp.exp(s_tail - top), 0.0)
    e_new = jnp.where(ok_new, jnp.exp(s_new - top), 0.0)
    total = e_win.sum(-1, keepdims=True) + e_tail.sum(-1, keepdims=True) + e_new.sum(-1, keepdims=True)
    p_win = (e_win / total).astype(jnp.bfloat16).astype(jnp.float32)
    p_tail = (e_tail / total).astype(jnp.bfloat16).astype(jnp.float32)
    p_new = (e_new / total).astype(jnp.bfloat16).astype(jnp.float32)
    out = jnp.einsum('sthk,kd->sthd', p_win, wv)
    out = out + jnp.einsum('sthj,sjd->sthd', p_tail, tv)
    out = out + jnp.einsum('sthu,sud->sthd', p_new, nv)
    return out.reshape(count, 2, -1).astype(jnp.bfloat16)

def extend(tails, fresh, tlen):
    rows = jnp.arange(tails.shape[1], dtype=jnp.int32)[None, :, None]
    lead = tlen[:, None, None]
    out = jnp.where(rows == lead, fresh[:, 0][:, None, :], tails)
    return jnp.where(rows == lead + 1, fresh[:, 1][:, None, :], out)

def rms_scale(values):
    return values * lax.rsqrt(lax.optimization_barrier(jnp.mean(values * values, axis=-1, keepdims=True)) + 1e-06)

def reference(queries, new_kv, residual, prompt_kv, tail_kv, page_pool, page_holder, serve_slot, prompt_len, tail_len, w_out, norm_mlp, w_gate, w_up, w_down, norm_final, w_score):
    samp_dev = SAMPLES // N_MLP
    rows = WIN + samp_dev * TAIL
    holder = page_holder.reshape(N_REQ, N_MLP, N_REQ)
    r_idx = jnp.arange(N_REQ, dtype=jnp.int32)[:, None, None]
    m_idx = jnp.arange(N_MLP, dtype=jnp.int32)[None, :, None]
    slot = serve_slot.reshape(N_REQ, N_MLP, N_REQ)[holder, m_idx, r_idx]
    flat = ((holder * N_MLP + m_idx) * N_REQ + slot).astype(jnp.int32)
    fetched = page_pool[flat].reshape(N_REQ, N_MLP, rows, 2 * HD)

    def one(items):
        q_r, n_r, p_r, t_r, f_r, pl_r, tl_r = items
        first = attend(q_r[0], n_r[0], p_r, t_r, pl_r[0], tl_r[0])
        q_b = q_r[1].reshape(N_MLP, samp_dev, 2, H * HD)
        n_b = n_r[1].reshape(N_MLP, samp_dev, 2, 2 * HD)
        tl_b = tl_r[1].reshape(N_MLP, samp_dev)
        wins = f_r[:, :WIN]
        tls = f_r[:, WIN:].reshape(N_MLP, samp_dev, TAIL, 2 * HD)
        second = jax.vmap(attend, in_axes=(0, 0, 0, 0, None, 0))(q_b, n_b, wins, tls, pl_r[1], tl_b)
        second = second.reshape(SAMPLES, 2, H * HD)
        tails_a = extend(t_r, n_r[0], tl_r[0])
        tails_b = extend(tls.reshape(SAMPLES, TAIL, 2 * HD), n_r[1], tl_r[1])
        return (jnp.stack([first, second]), jnp.stack([tails_a, tails_b]))
    attn, tails_out = lax.map(one, (queries, new_kv, prompt_kv, tail_kv, fetched, prompt_len, tail_len))
    mixed = jnp.dot(attn.reshape(-1, H * HD), w_out, preferred_element_type=jnp.float32)
    h1 = (residual.reshape(-1, D).astype(jnp.float32) + mixed).astype(jnp.bfloat16)
    normed = (rms_scale(h1.astype(jnp.float32)) * norm_mlp).astype(jnp.bfloat16)
    gate = jnp.dot(normed, w_gate, preferred_element_type=jnp.float32)
    up = jnp.dot(normed, w_up, preferred_element_type=jnp.float32)
    act = (jax.nn.gelu(gate, approximate=True) * up).astype(jnp.bfloat16)
    h2 = h1.astype(jnp.float32) + jnp.dot(act, w_down, preferred_element_type=jnp.float32)
    scores = lax.optimization_barrier(jnp.sum(rms_scale(h2) * norm_final * w_score, axis=-1))
    return (scores.reshape(N_REQ, 2, SAMPLES, 2), h2.astype(jnp.bfloat16).reshape(N_REQ, 2, SAMPLES, 2, D), tails_out)
```

```python
import functools

import jax
import jax.numpy as jnp
from jax import lax
from jax.experimental import pallas as pl
from jax.experimental.pallas import tpu as pltpu
from jax.sharding import PartitionSpec as P

F32 = jnp.float32
BF16 = jnp.bfloat16
MESH = pl.DeviceIdType.MESH
HEAD = 128
LANES = 128


def page_order(count):
    half = count // 2
    return sorted(range(1, count), key=lambda d: (abs(d - half), d))


def block_kernel(
    n_req,
    n_mlp,
    exchange,
    holder_ref,
    slot_ref,
    plen_ref,
    tlen_ref,
    q_ref,
    new_ref,
    res_ref,
    norm_mlp_ref,
    norm_final_ref,
    w_score_ref,
    pool_hbm,
    prompt_hbm,
    tail_hbm,
    w_out_hbm,
    w_gate_hbm,
    w_up_hbm,
    w_down_hbm,
    scores_ref,
    hidden_ref,
    tails_ref,
    pool,
    outgoing,
    arrived,
    kv,
    w_out,
    w_gate,
    w_up,
    w_down,
    qf,
    nf,
    rf,
    attn_send,
    attn_recv,
    mix_own,
    mix_send,
    mix_recv,
    normed,
    down_own,
    down_send,
    down_recv,
    h1_own,
    load_sem,
    page_send_sem,
    page_recv_sem,
    mlp_send_sem,
    mlp_recv_sem,
):
    samp = q_ref.shape[2]
    width = res_ref.shape[-1]
    rows = 2 * samp * 2
    half = samp * 2
    win = prompt_hbm.shape[0]
    tail_rows = tails_ref.shape[3]
    fetched_rows = win + samp * tail_rows
    kv_rows = kv.shape[1]
    heads = q_ref.shape[-1] // HEAD
    block = w_out_hbm.shape[0]
    hidden = w_gate_hbm.shape[1]
    r = lax.axis_index("req")
    m = lax.axis_index("mlp")

    barrier = pltpu.get_barrier_semaphore()
    peers = n_mlp - 1
    for d in range(1, n_mlp):
        pl.semaphore_signal(
            barrier, inc=1, device_id={"mlp": lax.rem(m + d, n_mlp)}, device_id_type=MESH
        )
    if exchange:
        peers += n_req - 1
        for d in range(1, n_req):
            pl.semaphore_signal(
                barrier, inc=1, device_id={"req": lax.rem(r + d, n_req)}, device_id_type=MESH
            )

    loads = []

    def load(src, dst):
        copy = pltpu.make_async_copy(src, dst, load_sem.at[len(loads)])
        copy.start()
        loads.append(copy)
        return copy

    pool_load = load(pool_hbm, pool) if exchange else load(pool_hbm, kv.at[1, 0:fetched_rows])
    prompt_load = load(prompt_hbm, kv.at[0, 0:win])
    tail_load = load(tail_hbm, kv.at[0, win:fetched_rows])
    w_out_load = load(w_out_hbm, w_out)
    w_gate_load = load(w_gate_hbm, w_gate)
    w_up_load = load(w_up_hbm, w_up)
    w_down_load = load(w_down_hbm, w_down)

    pages = []
    if exchange:
        page = pool.shape[1]
        pool_load.wait()
        for d in page_order(n_req):
            target = lax.rem(r + d, n_req)
            outgoing[target] = pool[slot_ref[0, target]]
        pl.semaphore_wait(barrier, peers)
        for d in page_order(n_req):
            target = lax.rem(r + d, n_req)
            copy = pltpu.make_async_remote_copy(
                src_ref=outgoing.at[target],
                dst_ref=arrived.at[r],
                send_sem=page_send_sem.at[d],
                recv_sem=page_recv_sem.at[d],
                device_id={"req": target},
                device_id_type=MESH,
            )
            copy.start()
            pages.append(copy)
        arrived[r] = pool[slot_ref[0, r]]
    else:
        pl.semaphore_wait(barrier, peers)

    for i in range(2 * samp):
        q, s = divmod(i, samp)
        qf[2 * i : 2 * i + 2, :] = q_ref[0, q, s].astype(F32)
        nf[2 * i : 2 * i + 2, :] = new_ref[0, q, s].astype(F32)
        rf[2 * i : 2 * i + 2, :] = res_ref[0, q, s].astype(F32)
    fresh = jnp.concatenate(
        [nf[...], jnp.zeros((kv_rows - fetched_rows - rows, nf.shape[1]), F32)], axis=0
    ).astype(BF16)
    kv[0, fetched_rows:kv_rows, :] = fresh
    kv[1, fetched_rows:kv_rows, :] = fresh

    def attend(q):
        own = qf[q * half : (q + 1) * half, :]
        query = jnp.concatenate(
            [own[:, h * HEAD : (h + 1) * HEAD] for h in range(heads)], axis=0
        ).astype(BF16)
        count = heads * half
        scores = lax.dot_general(
            query,
            kv[q, :, 0:HEAD],
            (((1,), (1,)), ((), ())),
            preferred_element_type=F32,
        ) * (1.0 / jnp.sqrt(F32(HEAD)))
        line = lax.broadcasted_iota(jnp.int32, (count, 1), 0) % half
        token = line % 2
        sample = line // 2
        length = jnp.zeros((count, 1), jnp.int32)
        for s in range(samp):
            length = jnp.where(sample == s, tlen_ref[0, q, s], length)
        first = jnp.maximum(win - plen_ref[0, q], length + token + 1)
        col = lax.broadcasted_iota(jnp.int32, (1, win), 1)
        s_win = jnp.where(col >= first, scores[:, 0:win], -1e30)
        col = lax.broadcasted_iota(jnp.int32, (1, samp * tail_rows), 1)
        place = col - sample * tail_rows
        s_tail = jnp.where(
            (place >= 0) & (place < length), scores[:, win:fetched_rows], -1e30
        )
        col = lax.broadcasted_iota(jnp.int32, (1, kv_rows - fetched_rows), 1)
        place = col - (q * half + sample * 2)
        s_new = jnp.where(
            (place >= 0) & (place <= token), scores[:, fetched_rows:kv_rows], -1e30
        )
        scores = jnp.concatenate([s_win, s_tail, s_new], axis=1)
        top = jnp.max(scores, axis=1, keepdims=True)
        e = jnp.exp(scores - top)
        total = jnp.sum(e, axis=1, keepdims=True)
        out = jnp.dot(e.astype(BF16), kv[q, :, HEAD : 2 * HEAD], preferred_element_type=F32)
        return out / total

    def write_tails(q):
        line = lax.broadcasted_iota(jnp.int32, (tail_rows, 1), 0)
        for s in range(samp):
            i = (q * samp + s) * 2
            lead = tlen_ref[0, q, s]
            old = kv[q, win + s * tail_rows : win + (s + 1) * tail_rows, :].astype(F32)
            out = jnp.where(line == lead, nf[i : i + 1, :], old)
            out = jnp.where(line == lead + 1, nf[i + 1 : i + 2, :], out)
            tails_ref[0, q, s] = out.astype(BF16)

    prompt_load.wait()
    tail_load.wait()
    first = attend(0)
    write_tails(0)

    if exchange:
        for copy in pages:
            copy.wait_recv()
        for p in range(n_req):
            kv[1, p * page : (p + 1) * page, :] = arrived[holder_ref[0, p]]
    else:
        pool_load.wait()
    second = attend(1)

    def pieces(out, j):
        per = block // HEAD
        return jnp.concatenate(
            [out[(j * per + h) * half : (j * per + h + 1) * half, :] for h in range(per)], axis=1
        )

    for j in range(n_mlp):
        attn_send[j] = jnp.concatenate([pieces(first, j), pieces(second, j)], axis=0).astype(BF16)

    def send_all(phase, source, place):
        copies = []
        for d in range(1, n_mlp):
            target = lax.rem(m + d, n_mlp)
            copy = pltpu.make_async_remote_copy(
                src_ref=source(target),
                dst_ref=place(d),
                send_sem=mlp_send_sem.at[phase, d],
                recv_sem=mlp_recv_sem.at[phase, d],
                device_id={"mlp": target},
                device_id_type=MESH,
            )
            copy.start()
            copies.append(copy)
        return copies

    gathered = send_all(0, lambda t: attn_send.at[t], lambda d: attn_recv.at[m])
    attn_recv[m] = attn_send[m]
    write_tails(1)
    w_out_load.wait()
    for copy in gathered:
        copy.wait_recv()
    every = jnp.concatenate([attn_recv[j] for j in range(n_mlp)], axis=0)
    mixed = jnp.dot(every, w_out[...], preferred_element_type=F32)
    for j in range(n_mlp):
        part = mixed[j * rows : (j + 1) * rows, :]
        mix_own[j] = part
        mix_send[j] = part.astype(BF16)
    summed = send_all(1, lambda t: mix_send.at[t], lambda d: mix_recv.at[d])
    total = rf[...] + mix_own[m]
    for d in range(1, n_mlp):
        summed[d - 1].wait_recv()
        total = total + mix_recv[d].astype(F32)
    h1 = total.astype(BF16).astype(F32)
    h1_own[...] = h1
    scale = lax.rsqrt(jnp.mean(h1 * h1, axis=-1, keepdims=True) + 1e-06)
    normed[m] = (h1 * scale * norm_mlp_ref[...]).astype(BF16)
    spread = send_all(2, lambda t: normed.at[m], lambda d: normed.at[m])
    w_gate_load.wait()
    w_up_load.wait()
    w_down_load.wait()
    for copy in spread:
        copy.wait_recv()
    every = jnp.concatenate([normed[j] for j in range(n_mlp)], axis=0)
    step = 3 * LANES if hidden % (3 * LANES) == 0 else hidden
    acts = []
    for c in range(0, hidden, step):
        gate = jnp.dot(every, w_gate[:, c : c + step], preferred_element_type=F32)
        up = jnp.dot(every, w_up[:, c : c + step], preferred_element_type=F32)
        acts.append((jax.nn.gelu(gate, approximate=True) * up).astype(BF16))
    act = jnp.concatenate(acts, axis=1)
    down = jnp.dot(act, w_down[...], preferred_element_type=F32)
    for j in range(n_mlp):
        part = down[j * rows : (j + 1) * rows, :]
        down_own[j] = part
        down_send[j] = part.astype(BF16)
    last = send_all(3, lambda t: down_send.at[t], lambda d: down_recv.at[d])
    h2 = h1_own[...] + down_own[m]
    for d in range(1, n_mlp):
        last[d - 1].wait_recv()
        h2 = h2 + down_recv[d].astype(F32)
    scale = lax.rsqrt(jnp.mean(h2 * h2, axis=-1, keepdims=True) + 1e-06)
    scores_ref[...] = jnp.sum(
        h2 * scale * norm_final_ref[...] * w_score_ref[...], axis=-1, keepdims=True
    )
    rf[...] = h2
    for i in range(2 * samp):
        q, s = divmod(i, samp)
        hidden_ref[0, q, s] = rf[2 * i : 2 * i + 2, :].astype(BF16)
    for copy in pages + gathered + summed + spread + last:
        copy.wait_send()


def on_device(
    n_req,
    n_mlp,
    queries,
    new_kv,
    residual,
    prompt_kv,
    tail_kv,
    page_pool,
    page_holder,
    serve_slot,
    prompt_len,
    tail_len,
    w_out,
    norm_mlp,
    w_gate,
    w_up,
    w_down,
    norm_final,
    w_score,
):
    samp = queries.shape[2]
    width = residual.shape[-1]
    kv_width = new_kv.shape[-1]
    win = prompt_kv.shape[1]
    tail_rows = tail_kv.shape[2]
    fetched_rows = win + samp * tail_rows
    page = page_pool.shape[1]
    rows = 4 * samp
    block = w_out.shape[0]
    hidden = w_gate.shape[1]
    exchange = page % 16 == 0
    if exchange:
        pool = page_pool
        page_bufs = (n_req, page, kv_width)
    else:
        outgoing = jnp.take(page_pool, serve_slot[0], axis=0)
        arrived = lax.all_to_all(outgoing, "req", split_axis=0, concat_axis=0, tiled=True)
        pool = jnp.take(arrived, page_holder[0], axis=0).reshape(-1, kv_width)
        page_bufs = (1, 16, kv_width)
    pool_buf = page_pool.shape if exchange else page_bufs
    vmem = pl.BlockSpec(memory_space=pltpu.VMEM)
    smem = pl.BlockSpec(memory_space=pltpu.SMEM)
    hbm = pl.BlockSpec(memory_space=pl.ANY)
    sems = n_req if exchange else 1
    scores, hidden_out, tails_out = pl.pallas_call(
        functools.partial(block_kernel, n_req, n_mlp, exchange),
        out_shape=(
            jax.ShapeDtypeStruct((rows, 1), F32),
            jax.ShapeDtypeStruct(residual.shape, BF16),
            jax.ShapeDtypeStruct((1, 2, samp, tail_rows, kv_width), BF16),
        ),
        in_specs=[smem] * 4 + [vmem] * 6 + [hbm] * 7,
        out_specs=(vmem, vmem, vmem),
        scratch_shapes=[
            pltpu.VMEM(pool_buf, BF16),
            pltpu.VMEM(page_bufs, BF16),
            pltpu.VMEM(page_bufs, BF16),
            pltpu.VMEM((2, fetched_rows + LANES, kv_width), BF16),
            pltpu.VMEM(w_out.shape, BF16),
            pltpu.VMEM(w_gate.shape, BF16),
            pltpu.VMEM(w_up.shape, BF16),
            pltpu.VMEM(w_down.shape, BF16),
            pltpu.VMEM((rows, queries.shape[-1]), F32),
            pltpu.VMEM((rows, kv_width), F32),
            pltpu.VMEM((rows, width), F32),
            pltpu.VMEM((n_mlp, rows, block), BF16),
            pltpu.VMEM((n_mlp, rows, block), BF16),
            pltpu.VMEM((n_mlp, rows, width), F32),
            pltpu.VMEM((n_mlp, rows, width), BF16),
            pltpu.VMEM((n_mlp, rows, width), BF16),
            pltpu.VMEM((n_mlp, rows, width), BF16),
            pltpu.VMEM((n_mlp, rows, width), F32),
            pltpu.VMEM((n_mlp, rows, width), BF16),
            pltpu.VMEM((n_mlp, rows, width), BF16),
            pltpu.VMEM((rows, width), F32),
            pltpu.SemaphoreType.DMA((7,)),
            pltpu.SemaphoreType.DMA((sems,)),
            pltpu.SemaphoreType.DMA((sems,)),
            pltpu.SemaphoreType.DMA((4, n_mlp)),
            pltpu.SemaphoreType.DMA((4, n_mlp)),
        ],
        compiler_params=pltpu.CompilerParams(
            collective_id=0, has_side_effects=True, vmem_limit_bytes=48 * 1024 * 1024
        ),
        cost_estimate=pl.CostEstimate(
            flops=2 * n_mlp * rows * width * (block + 3 * hidden),
            bytes_accessed=2 * width * (block + 3 * hidden),
            transcendentals=0,
        ),
    )(
        page_holder,
        serve_slot,
        prompt_len,
        tail_len,
        queries,
        new_kv,
        residual,
        norm_mlp.reshape(1, -1),
        norm_final.reshape(1, -1),
        w_score.reshape(1, -1),
        pool,
        prompt_kv.reshape(win, kv_width),
        tail_kv.reshape(samp * tail_rows, kv_width),
        w_out,
        w_gate,
        w_up,
        w_down,
    )
    return scores.reshape(1, 2, samp, 2), hidden_out, tails_out


def solution(mesh):
    placed = (
        P("req", None, "mlp", None, None),
        P("req", None, "mlp", None, None),
        P("req", None, "mlp", None, None),
        P("req", None, None),
        P("req", "mlp", None, None),
        P(("req", "mlp"), None, None),
        P(("req", "mlp"), None),
        P(("req", "mlp"), None),
        P("req", None),
        P("req", None, "mlp"),
        P("mlp", None),
        P(),
        P(None, "mlp"),
        P(None, "mlp"),
        P("mlp", None),
        P(),
        P(),
    )
    return jax.shard_map(
        functools.partial(on_device, mesh.shape["req"], mesh.shape["mlp"]),
        mesh=mesh,
        in_specs=placed,
        out_specs=(
            P("req", None, "mlp", None),
            P("req", None, "mlp", None, None),
            P("req", None, "mlp", None, None),
        ),
        check_vma=False,
    )
```

```python
import functools

import jax
import jax.numpy as jnp
from jax import lax
from jax.experimental import pallas as pl
from jax.experimental.pallas import tpu as pltpu
from jax.sharding import PartitionSpec as P

F32 = jnp.float32
BF16 = jnp.bfloat16
MESH = pl.DeviceIdType.MESH
HEAD = 128
LANES = 128


def page_order(count):
    half = count // 2
    return sorted(range(1, count), key=lambda d: (abs(d - half), d))


def block_kernel(
    n_req,
    n_mlp,
    exchange,
    holder_hbm,
    slot_hbm,
    plen_hbm,
    tlen_hbm,
    q_hbm,
    new_hbm,
    res_hbm,
    norm_mlp_hbm,
    norm_final_hbm,
    w_score_hbm,
    pool_hbm,
    prompt_hbm,
    tail_hbm,
    w_out_hbm,
    w_gate_hbm,
    w_up_hbm,
    w_down_hbm,
    scores_ref,
    hidden_ref,
    tails_ref,
    holder_ref,
    slot_ref,
    plen_ref,
    tlen_ref,
    q_ref,
    new_ref,
    res_ref,
    norm_mlp_ref,
    norm_final_ref,
    w_score_ref,
    pool,
    outgoing,
    arrived,
    kv,
    w_out,
    w_gate,
    w_up,
    w_down,
    qf,
    nf,
    rf,
    attn_send,
    attn_recv,
    mix_own,
    mix_send,
    mix_recv,
    normed,
    down_own,
    down_send,
    down_recv,
    h1_own,
    load_sem,
    page_send_sem,
    page_recv_sem,
    mlp_send_sem,
    mlp_recv_sem,
    down_send_sem,
    down_recv_sem,
):
    samp = q_ref.shape[2]
    width = res_ref.shape[-1]
    rows = 2 * samp * 2
    half = samp * 2
    win = prompt_hbm.shape[0]
    tail_rows = tails_ref.shape[3]
    fetched_rows = win + samp * tail_rows
    kv_rows = kv.shape[1]
    heads = q_ref.shape[-1] // HEAD
    block = w_out_hbm.shape[0]
    hidden = w_gate_hbm.shape[1]
    cut = width // 2
    chunks = down_send.shape[0]
    r = lax.axis_index("req")
    m = lax.axis_index("mlp")

    barrier = pltpu.get_barrier_semaphore()
    peers = n_mlp - 1
    for d in range(1, n_mlp):
        pl.semaphore_signal(
            barrier, inc=1, device_id={"mlp": lax.rem(m + d, n_mlp)}, device_id_type=MESH
        )
    if exchange:
        peers += n_req - 1
        for d in range(1, n_req):
            pl.semaphore_signal(
                barrier, inc=1, device_id={"req": lax.rem(r + d, n_req)}, device_id_type=MESH
            )

    loads = []

    def load(src, dst):
        copy = pltpu.make_async_copy(src, dst, load_sem.at[len(loads)])
        copy.start()
        loads.append(copy)
        return copy

    slot_load = load(slot_hbm, slot_ref)
    pool_load = load(pool_hbm, pool) if exchange else load(pool_hbm, kv.at[1, 0:fetched_rows])
    small = [
        load(holder_hbm, holder_ref),
        load(plen_hbm, plen_ref),
        load(tlen_hbm, tlen_ref),
        load(q_hbm, q_ref),
        load(new_hbm, new_ref),
        load(res_hbm, res_ref),
        load(norm_mlp_hbm, norm_mlp_ref),
        load(norm_final_hbm, norm_final_ref),
        load(w_score_hbm, w_score_ref),
        load(prompt_hbm, kv.at[0, 0:win]),
        load(tail_hbm, kv.at[0, win:fetched_rows]),
    ]
    w_out_load = load(w_out_hbm, w_out)
    w_gate_load = load(w_gate_hbm, w_gate)
    w_up_load = load(w_up_hbm, w_up)
    w_down_load = load(w_down_hbm, w_down)

    pages = []
    slot_load.wait()
    if exchange:
        page = pool.shape[1]
        pool_load.wait()
        for d in page_order(n_req):
            target = lax.rem(r + d, n_req)
            outgoing[target] = pool[slot_ref[0, target]]
        pl.semaphore_wait(barrier, peers)
        for d in page_order(n_req):
            target = lax.rem(r + d, n_req)
            copy = pltpu.make_async_remote_copy(
                src_ref=outgoing.at[target],
                dst_ref=arrived.at[r],
                send_sem=page_send_sem.at[d],
                recv_sem=page_recv_sem.at[d],
                device_id={"req": target},
                device_id_type=MESH,
            )
            copy.start()
            pages.append(copy)
        arrived[r] = pool[slot_ref[0, r]]
    else:
        pl.semaphore_wait(barrier, peers)

    for copy in small:
        copy.wait()
    for i in range(2 * samp):
        q, s = divmod(i, samp)
        qf[2 * i : 2 * i + 2, :] = q_ref[0, q, s].astype(F32)
        nf[2 * i : 2 * i + 2, :] = new_ref[0, q, s].astype(F32)
        rf[2 * i : 2 * i + 2, :] = res_ref[0, q, s].astype(F32)
    fresh = jnp.concatenate(
        [nf[...], jnp.zeros((kv_rows - fetched_rows - rows, nf.shape[1]), F32)], axis=0
    ).astype(BF16)
    kv[0, fetched_rows:kv_rows, :] = fresh
    kv[1, fetched_rows:kv_rows, :] = fresh

    def attend(q):
        own = qf[q * half : (q + 1) * half, :]
        query = jnp.concatenate(
            [own[:, h * HEAD : (h + 1) * HEAD] for h in range(heads)], axis=0
        ).astype(BF16)
        count = heads * half
        scores = lax.dot_general(
            query,
            kv[q, :, 0:HEAD],
            (((1,), (1,)), ((), ())),
            preferred_element_type=F32,
        ) * (1.0 / jnp.sqrt(F32(HEAD)))
        line = lax.broadcasted_iota(jnp.int32, (count, 1), 0) % half
        token = line % 2
        sample = line // 2
        length = jnp.zeros((count, 1), jnp.int32)
        for s in range(samp):
            length = jnp.where(sample == s, tlen_ref[0, q, s], length)
        first = jnp.maximum(win - plen_ref[0, q], length + token + 1)
        col = lax.broadcasted_iota(jnp.int32, (1, win), 1)
        s_win = jnp.where(col >= first, scores[:, 0:win], -1e30)
        col = lax.broadcasted_iota(jnp.int32, (1, samp * tail_rows), 1)
        place = col - sample * tail_rows
        s_tail = jnp.where(
            (place >= 0) & (place < length), scores[:, win:fetched_rows], -1e30
        )
        col = lax.broadcasted_iota(jnp.int32, (1, kv_rows - fetched_rows), 1)
        place = col - (q * half + sample * 2)
        s_new = jnp.where(
            (place >= 0) & (place <= token), scores[:, fetched_rows:kv_rows], -1e30
        )
        scores = jnp.concatenate([s_win, s_tail, s_new], axis=1)
        top = jnp.max(scores, axis=1, keepdims=True)
        e = jnp.exp(scores - top)
        total = jnp.sum(e, axis=1, keepdims=True)
        out = jnp.dot(e.astype(BF16), kv[q, :, HEAD : 2 * HEAD], preferred_element_type=F32)
        return out / total

    def write_tails(q):
        line = lax.broadcasted_iota(jnp.int32, (tail_rows, 1), 0)
        for s in range(samp):
            i = (q * samp + s) * 2
            lead = tlen_ref[0, q, s]
            old = kv[q, win + s * tail_rows : win + (s + 1) * tail_rows, :].astype(F32)
            out = jnp.where(line == lead, nf[i : i + 1, :], old)
            out = jnp.where(line == lead + 1, nf[i + 1 : i + 2, :], out)
            tails_ref[0, q, s] = out.astype(BF16)

    def send_all(source, place, send_sem, recv_sem):
        copies = []
        for d in range(1, n_mlp):
            target = lax.rem(m + d, n_mlp)
            copy = pltpu.make_async_remote_copy(
                src_ref=source(target),
                dst_ref=place(d),
                send_sem=send_sem(d),
                recv_sem=recv_sem(d),
                device_id={"mlp": target},
                device_id_type=MESH,
            )
            copy.start()
            copies.append(copy)
        return copies

    def send_phase(phase, q, source, place):
        return send_all(
            source,
            place,
            lambda d: mlp_send_sem.at[phase, q, d],
            lambda d: mlp_recv_sem.at[phase, q, d],
        )

    def fold(x):
        return jnp.concatenate([x[:, :cut], x[:, cut:]], axis=0).astype(BF16)

    def unfold(x):
        x = x.astype(F32)
        return jnp.concatenate([x[:half], x[half:]], axis=1)

    per = block // HEAD

    def send_heads(q, out):
        for j in range(n_mlp):
            attn_send[q, j] = jnp.concatenate(
                [out[(j * per + h) * half : (j * per + h + 1) * half, :] for h in range(per)],
                axis=1,
            )
        copies = send_phase(
            0, q, lambda t: attn_send.at[q, t], lambda d: attn_recv.at[q, m]
        )
        attn_recv[q, m] = attn_send[q, m]
        return copies

    def project(q, copies):
        for copy in copies:
            copy.wait_recv()
        every = jnp.concatenate([attn_recv[q, j] for j in range(n_mlp)], axis=0).astype(BF16)
        mixed = jnp.dot(every, w_out[...], preferred_element_type=F32)
        for j in range(n_mlp):
            part = mixed[j * half : (j + 1) * half, :]
            mix_own[q, j] = part
            mix_send[q, j] = fold(part)
        return send_phase(1, q, lambda t: mix_send.at[q, t], lambda d: mix_recv.at[q, d])

    def normalise(q, copies):
        total = rf[q * half : (q + 1) * half, :] + mix_own[q, m]
        for copy in copies:
            copy.wait_recv()
        for d in range(1, n_mlp):
            total = total + unfold(mix_recv[q, d])
        h1 = total.astype(BF16).astype(F32)
        h1_own[q * half : (q + 1) * half, :] = h1
        scale = lax.rsqrt(jnp.mean(h1 * h1, axis=-1, keepdims=True) + 1e-06)
        normed[q, m] = fold(h1 * scale * norm_mlp_ref[...].reshape(1, width))
        return send_phase(2, q, lambda t: normed.at[q, m], lambda d: normed.at[q, m])

    done = []
    heads_0 = send_heads(0, attend(0))
    write_tails(0)
    w_out_load.wait()
    sums_0 = project(0, heads_0)
    rows_0 = normalise(0, sums_0)

    if exchange:
        for copy in pages:
            copy.wait_recv()
        for p in range(n_req):
            kv[1, p * page : (p + 1) * page, :] = arrived[holder_ref[0, p]]
    else:
        pool_load.wait()
    heads_1 = send_heads(1, attend(1))
    write_tails(1)
    sums_1 = project(1, heads_1)
    w_gate_load.wait()
    w_up_load.wait()
    w_down_load.wait()
    rows_1 = normalise(1, sums_1)
    for copy in rows_0 + rows_1:
        copy.wait_recv()
    every = jnp.concatenate(
        [unfold(normed[q, j]) for j in range(n_mlp) for q in range(2)], axis=0
    ).astype(BF16)
    acts = []
    for c in range(0, hidden, 2 * LANES):
        end = min(c + 2 * LANES, hidden)
        gate = jnp.dot(every, w_gate[:, c:end], preferred_element_type=F32)
        up = jnp.dot(every, w_up[:, c:end], preferred_element_type=F32)
        acts.append((jax.nn.gelu(gate, approximate=True) * up).astype(BF16))
    act = jnp.concatenate(acts, axis=1)
    span = width // chunks
    last = []
    for c in range(chunks):
        down = jnp.dot(act, w_down[:, c * span : (c + 1) * span], preferred_element_type=F32)
        for j in range(n_mlp):
            part = down[j * rows : (j + 1) * rows, :]
            down_own[c, j] = part
            down_send[c, j] = part.astype(BF16)
        last.append(
            send_all(
                lambda t: down_send.at[c, t],
                lambda d: down_recv.at[c, d],
                lambda d: down_send_sem.at[c, d],
                lambda d: down_recv_sem.at[c, d],
            )
        )
    parts = []
    for c in range(chunks):
        part = h1_own[:, c * span : (c + 1) * span] + down_own[c, m]
        for d in range(1, n_mlp):
            last[c][d - 1].wait_recv()
            part = part + down_recv[c, d].astype(F32)
        parts.append(part)
    h2 = jnp.concatenate(parts, axis=1)
    scale = lax.rsqrt(jnp.mean(h2 * h2, axis=-1, keepdims=True) + 1e-06)
    gain = (norm_final_ref[...] * w_score_ref[...]).reshape(1, width)
    sums = jnp.sum(h2 * scale * gain, axis=-1, keepdims=True)
    col = lax.broadcasted_iota(jnp.int32, (rows, 2), 1)
    line = lax.broadcasted_iota(jnp.int32, (rows, 2), 0)
    paired = jnp.where(line % 2 == col, sums, 0.0)
    rf[...] = h2
    for i in range(2 * samp):
        q, s = divmod(i, samp)
        hidden_ref[0, q, s] = rf[2 * i : 2 * i + 2, :].astype(BF16)
        scores_ref[0, q, s : s + 1, :] = jnp.sum(
            paired[2 * i : 2 * i + 2, :], axis=0, keepdims=True
        )
    for group in [pages, heads_0, sums_0, rows_0, heads_1, sums_1, rows_1] + last:
        for copy in group:
            copy.wait_send()


def on_device(
    n_req,
    n_mlp,
    queries,
    new_kv,
    residual,
    prompt_kv,
    tail_kv,
    page_pool,
    page_holder,
    serve_slot,
    prompt_len,
    tail_len,
    w_out,
    norm_mlp,
    w_gate,
    w_up,
    w_down,
    norm_final,
    w_score,
):
    samp = queries.shape[2]
    width = residual.shape[-1]
    kv_width = new_kv.shape[-1]
    win = prompt_kv.shape[1]
    tail_rows = tail_kv.shape[2]
    fetched_rows = win + samp * tail_rows
    page = page_pool.shape[1]
    rows = 4 * samp
    block = w_out.shape[0]
    hidden = w_gate.shape[1]
    exchange = page % 16 == 0
    if exchange:
        pool = page_pool
        page_bufs = (n_req, page, kv_width)
    else:
        outgoing = jnp.take(page_pool, serve_slot[0], axis=0)
        arrived = lax.all_to_all(outgoing, "req", split_axis=0, concat_axis=0, tiled=True)
        pool = jnp.take(arrived, page_holder[0], axis=0).reshape(-1, kv_width)
        page_bufs = (1, 16, kv_width)
    pool_buf = page_pool.shape if exchange else page_bufs
    vmem = pl.BlockSpec(memory_space=pltpu.VMEM)
    hbm = pl.BlockSpec(memory_space=pltpu.HBM)
    sems = n_req if exchange else 1
    chunks = 3
    scores, hidden_out, tails_out = pl.pallas_call(
        functools.partial(block_kernel, n_req, n_mlp, exchange),
        out_shape=(
            jax.ShapeDtypeStruct((1, 2, samp, 2), F32),
            jax.ShapeDtypeStruct(residual.shape, BF16),
            jax.ShapeDtypeStruct((1, 2, samp, tail_rows, kv_width), BF16),
        ),
        in_specs=[hbm] * 17,
        out_specs=(vmem, vmem, vmem),
        scratch_shapes=[
            pltpu.SMEM(page_holder.shape, jnp.int32),
            pltpu.SMEM(serve_slot.shape, jnp.int32),
            pltpu.SMEM(prompt_len.shape, jnp.int32),
            pltpu.SMEM(tail_len.shape, jnp.int32),
            pltpu.VMEM(queries.shape, BF16),
            pltpu.VMEM(new_kv.shape, BF16),
            pltpu.VMEM(residual.shape, BF16),
            pltpu.VMEM(norm_mlp.shape, F32),
            pltpu.VMEM(norm_final.shape, F32),
            pltpu.VMEM(w_score.shape, F32),
            pltpu.VMEM(pool_buf, BF16),
            pltpu.VMEM(page_bufs, BF16),
            pltpu.VMEM(page_bufs, BF16),
            pltpu.VMEM((2, fetched_rows + LANES, kv_width), BF16),
            pltpu.VMEM(w_out.shape, BF16),
            pltpu.VMEM(w_gate.shape, BF16),
            pltpu.VMEM(w_up.shape, BF16),
            pltpu.VMEM(w_down.shape, BF16),
            pltpu.VMEM((rows, queries.shape[-1]), F32),
            pltpu.VMEM((rows, kv_width), F32),
            pltpu.VMEM((rows, width), F32),
            pltpu.VMEM((2, n_mlp, rows // 2, block), F32),
            pltpu.VMEM((2, n_mlp, rows // 2, block), F32),
            pltpu.VMEM((2, n_mlp, rows // 2, width), F32),
            pltpu.VMEM((2, n_mlp, rows, width // 2), BF16),
            pltpu.VMEM((2, n_mlp, rows, width // 2), BF16),
            pltpu.VMEM((2, n_mlp, rows, width // 2), BF16),
            pltpu.VMEM((chunks, n_mlp, rows, width // chunks), F32),
            pltpu.VMEM((chunks, n_mlp, rows, width // chunks), BF16),
            pltpu.VMEM((chunks, n_mlp, rows, width // chunks), BF16),
            pltpu.VMEM((rows, width), F32),
            pltpu.SemaphoreType.DMA((17,)),
            pltpu.SemaphoreType.DMA((sems,)),
            pltpu.SemaphoreType.DMA((sems,)),
            pltpu.SemaphoreType.DMA((3, 2, n_mlp)),
            pltpu.SemaphoreType.DMA((3, 2, n_mlp)),
            pltpu.SemaphoreType.DMA((chunks, n_mlp)),
            pltpu.SemaphoreType.DMA((chunks, n_mlp)),
        ],
        compiler_params=pltpu.CompilerParams(
            collective_id=0, has_side_effects=True, vmem_limit_bytes=48 * 1024 * 1024
        ),
        cost_estimate=pl.CostEstimate(
            flops=2 * n_mlp * rows * width * (block + 3 * hidden),
            bytes_accessed=2 * width * (block + 3 * hidden),
            transcendentals=0,
        ),
    )(
        page_holder,
        serve_slot,
        prompt_len,
        tail_len,
        queries,
        new_kv,
        residual,
        norm_mlp,
        norm_final,
        w_score,
        pool,
        prompt_kv.reshape(win, kv_width),
        tail_kv.reshape(samp * tail_rows, kv_width),
        w_out,
        w_gate,
        w_up,
        w_down,
    )
    return scores, hidden_out, tails_out


def solution(mesh):
    placed = (
        P("req", None, "mlp", None, None),
        P("req", None, "mlp", None, None),
        P("req", None, "mlp", None, None),
        P("req", None, None),
        P("req", "mlp", None, None),
        P(("req", "mlp"), None, None),
        P(("req", "mlp"), None),
        P(("req", "mlp"), None),
        P("req", None),
        P("req", None, "mlp"),
        P("mlp", None),
        P(),
        P(None, "mlp"),
        P(None, "mlp"),
        P("mlp", None),
        P(),
        P(),
    )
    return jax.shard_map(
        functools.partial(on_device, mesh.shape["req"], mesh.shape["mlp"]),
        mesh=mesh,
        in_specs=placed,
        out_specs=(
            P("req", None, "mlp", None),
            P("req", None, "mlp", None, None),
            P("req", None, "mlp", None, None),
        ),
        check_vma=False,
    )
```

```python
import functools

import jax
import jax.numpy as jnp
from jax import lax
from jax.experimental import pallas as pl
from jax.experimental.pallas import tpu as pltpu
from jax.sharding import PartitionSpec as P

F32 = jnp.float32
BF16 = jnp.bfloat16
MESH = pl.DeviceIdType.MESH
HEAD = 128
LANES = 128


def page_order(count):
    half = count // 2
    return sorted(range(1, count), key=lambda d: (abs(d - half), d))


def block_kernel(
    n_req,
    n_mlp,
    exchange,
    holder_hbm,
    slot_hbm,
    plen_hbm,
    tlen_hbm,
    q_hbm,
    new_hbm,
    res_hbm,
    norm_mlp_hbm,
    norm_final_hbm,
    w_score_hbm,
    pool_hbm,
    prompt_hbm,
    tail_hbm,
    w_out_hbm,
    w_gate_hbm,
    w_up_hbm,
    w_down_hbm,
    scores_hbm,
    hidden_hbm,
    tails_hbm,
    scores_ref,
    hidden_ref,
    tails_ref,
    holder_ref,
    slot_ref,
    plen_ref,
    tlen_ref,
    q_ref,
    new_ref,
    res_ref,
    norm_mlp_ref,
    norm_final_ref,
    w_score_ref,
    pool,
    outgoing,
    arrived,
    kv,
    w_out,
    w_gate,
    w_up,
    w_down,
    qf,
    nf,
    rf,
    attn_send,
    attn_recv,
    mix_own,
    mix_send,
    mix_recv,
    normed,
    down_own,
    down_send,
    down_recv,
    h1_own,
    load_sem,
    page_send_sem,
    page_recv_sem,
    mlp_send_sem,
    mlp_recv_sem,
    down_send_sem,
    down_recv_sem,
    store_sem,
):
    samp = q_ref.shape[2]
    width = res_ref.shape[-1]
    rows = 2 * samp * 2
    half = samp * 2
    win = prompt_hbm.shape[0]
    tail_rows = tails_ref.shape[3]
    fetched_rows = win + samp * tail_rows
    kv_rows = kv.shape[1]
    heads = q_ref.shape[-1] // HEAD
    block = w_out_hbm.shape[0]
    hidden = w_gate_hbm.shape[1]
    cut = width // 2
    chunks = down_send.shape[0]
    r = lax.axis_index("req")
    m = lax.axis_index("mlp")

    barrier = pltpu.get_barrier_semaphore()
    peers = n_mlp - 1
    for d in range(1, n_mlp):
        pl.semaphore_signal(
            barrier, inc=1, device_id={"mlp": lax.rem(m + d, n_mlp)}, device_id_type=MESH
        )
    if exchange:
        peers += n_req - 1
        for d in range(1, n_req):
            pl.semaphore_signal(
                barrier, inc=1, device_id={"req": lax.rem(r + d, n_req)}, device_id_type=MESH
            )

    loads = []

    def load(src, dst):
        copy = pltpu.make_async_copy(src, dst, load_sem.at[len(loads)])
        copy.start()
        loads.append(copy)
        return copy

    slot_load = load(slot_hbm, slot_ref)
    pool_load = load(pool_hbm, pool) if exchange else load(pool_hbm, kv.at[1, 0:fetched_rows])
    small = [
        load(holder_hbm, holder_ref),
        load(plen_hbm, plen_ref),
        load(tlen_hbm, tlen_ref),
        load(q_hbm, q_ref),
        load(new_hbm, new_ref),
        load(res_hbm, res_ref),
        load(norm_mlp_hbm, norm_mlp_ref),
        load(norm_final_hbm, norm_final_ref),
        load(w_score_hbm, w_score_ref),
        load(prompt_hbm, kv.at[0, 0:win]),
        load(tail_hbm, kv.at[0, win:fetched_rows]),
    ]
    w_out_load = load(w_out_hbm, w_out)
    w_gate_load = load(w_gate_hbm, w_gate)
    w_up_load = load(w_up_hbm, w_up)
    w_down_load = load(w_down_hbm, w_down)

    pages = []
    slot_load.wait()
    if exchange:
        page = pool.shape[1]
        pool_load.wait()
        for d in page_order(n_req):
            target = lax.rem(r + d, n_req)
            outgoing[target] = pool[slot_ref[0, target]]
        pl.semaphore_wait(barrier, peers)
        for d in page_order(n_req):
            target = lax.rem(r + d, n_req)
            copy = pltpu.make_async_remote_copy(
                src_ref=outgoing.at[target],
                dst_ref=arrived.at[r],
                send_sem=page_send_sem.at[d],
                recv_sem=page_recv_sem.at[d],
                device_id={"req": target},
                device_id_type=MESH,
            )
            copy.start()
            pages.append(copy)
        arrived[r] = pool[slot_ref[0, r]]
    else:
        pl.semaphore_wait(barrier, peers)

    for copy in small:
        copy.wait()
    for i in range(2 * samp):
        q, s = divmod(i, samp)
        qf[2 * i : 2 * i + 2, :] = q_ref[0, q, s].astype(F32)
        nf[2 * i : 2 * i + 2, :] = new_ref[0, q, s].astype(F32)
        rf[2 * i : 2 * i + 2, :] = res_ref[0, q, s].astype(F32)
    fresh = jnp.concatenate(
        [nf[...], jnp.zeros((kv_rows - fetched_rows - rows, nf.shape[1]), F32)], axis=0
    ).astype(BF16)
    kv[0, fetched_rows:kv_rows, :] = fresh
    kv[1, fetched_rows:kv_rows, :] = fresh

    def attend(q):
        own = qf[q * half : (q + 1) * half, :]
        query = jnp.concatenate(
            [own[:, h * HEAD : (h + 1) * HEAD] for h in range(heads)], axis=0
        ).astype(BF16)
        count = heads * half
        scores = lax.dot_general(
            query,
            kv[q, :, 0:HEAD],
            (((1,), (1,)), ((), ())),
            preferred_element_type=F32,
        ) * (1.0 / jnp.sqrt(F32(HEAD)))
        line = lax.broadcasted_iota(jnp.int32, (count, 1), 0) % half
        token = line % 2
        sample = line // 2
        length = jnp.zeros((count, 1), jnp.int32)
        for s in range(samp):
            length = jnp.where(sample == s, tlen_ref[0, q, s], length)
        first = jnp.maximum(win - plen_ref[0, q], length + token + 1)
        col = lax.broadcasted_iota(jnp.int32, (1, win), 1)
        s_win = jnp.where(col >= first, scores[:, 0:win], -1e30)
        col = lax.broadcasted_iota(jnp.int32, (1, samp * tail_rows), 1)
        place = col - sample * tail_rows
        s_tail = jnp.where(
            (place >= 0) & (place < length), scores[:, win:fetched_rows], -1e30
        )
        col = lax.broadcasted_iota(jnp.int32, (1, kv_rows - fetched_rows), 1)
        place = col - (q * half + sample * 2)
        s_new = jnp.where(
            (place >= 0) & (place <= token), scores[:, fetched_rows:kv_rows], -1e30
        )
        scores = jnp.concatenate([s_win, s_tail, s_new], axis=1)
        top = jnp.max(scores, axis=1, keepdims=True)
        e = jnp.exp(scores - top)
        total = jnp.sum(e, axis=1, keepdims=True)
        out = jnp.dot(e.astype(BF16), kv[q, :, HEAD : 2 * HEAD], preferred_element_type=F32)
        return out / total

    def write_tails(q):
        line = lax.broadcasted_iota(jnp.int32, (tail_rows, 1), 0)
        for s in range(samp):
            i = (q * samp + s) * 2
            lead = tlen_ref[0, q, s]
            old = kv[q, win + s * tail_rows : win + (s + 1) * tail_rows, :].astype(F32)
            out = jnp.where(line == lead, nf[i : i + 1, :], old)
            out = jnp.where(line == lead + 1, nf[i + 1 : i + 2, :], out)
            tails_ref[0, q, s] = out.astype(BF16)
        copy = pltpu.make_async_copy(tails_ref.at[0, q], tails_hbm.at[0, q], store_sem.at[q])
        copy.start()
        return copy

    def send_all(source, place, send_sem, recv_sem):
        copies = []
        for d in range(1, n_mlp):
            target = lax.rem(m + d, n_mlp)
            copy = pltpu.make_async_remote_copy(
                src_ref=source(target),
                dst_ref=place(d),
                send_sem=send_sem(d),
                recv_sem=recv_sem(d),
                device_id={"mlp": target},
                device_id_type=MESH,
            )
            copy.start()
            copies.append(copy)
        return copies

    def send_phase(phase, q, source, place):
        return send_all(
            source,
            place,
            lambda d: mlp_send_sem.at[phase, q, d],
            lambda d: mlp_recv_sem.at[phase, q, d],
        )

    def fold(x):
        return jnp.concatenate([x[:, :cut], x[:, cut:]], axis=0).astype(BF16)

    def unfold(x):
        x = x.astype(F32)
        return jnp.concatenate([x[:half], x[half:]], axis=1)

    per = block // HEAD

    def send_heads(q, out):
        for j in range(n_mlp):
            attn_send[q, j] = jnp.concatenate(
                [out[(j * per + h) * half : (j * per + h + 1) * half, :] for h in range(per)],
                axis=1,
            )
        copies = send_phase(
            0, q, lambda t: attn_send.at[q, t], lambda d: attn_recv.at[q, m]
        )
        attn_recv[q, m] = attn_send[q, m]
        return copies

    def project(q, copies):
        for copy in copies:
            copy.wait_recv()
        every = jnp.concatenate([attn_recv[q, j] for j in range(n_mlp)], axis=0).astype(BF16)
        mixed = jnp.dot(every, w_out[...], preferred_element_type=F32)
        for j in range(n_mlp):
            part = mixed[j * half : (j + 1) * half, :]
            mix_own[q, j] = part
            mix_send[q, j] = fold(part)
        return send_phase(1, q, lambda t: mix_send.at[q, t], lambda d: mix_recv.at[q, d])

    def normalise(q, copies):
        total = rf[q * half : (q + 1) * half, :] + mix_own[q, m]
        for copy in copies:
            copy.wait_recv()
        for d in range(1, n_mlp):
            total = total + unfold(mix_recv[q, d])
        h1 = total.astype(BF16).astype(F32)
        h1_own[q * half : (q + 1) * half, :] = h1
        scale = lax.rsqrt(jnp.mean(h1 * h1, axis=-1, keepdims=True) + 1e-06)
        normed[q, m] = fold(h1 * scale * norm_mlp_ref[...].reshape(1, width))
        return send_phase(2, q, lambda t: normed.at[q, m], lambda d: normed.at[q, m])

    done = []
    heads_0 = send_heads(0, attend(0))
    stores = [write_tails(0)]
    w_out_load.wait()
    sums_0 = project(0, heads_0)
    rows_0 = normalise(0, sums_0)

    if exchange:
        for copy in pages:
            copy.wait_recv()
        for p in range(n_req):
            kv[1, p * page : (p + 1) * page, :] = arrived[holder_ref[0, p]]
    else:
        pool_load.wait()
    heads_1 = send_heads(1, attend(1))
    stores.append(write_tails(1))
    sums_1 = project(1, heads_1)
    w_gate_load.wait()
    w_up_load.wait()
    w_down_load.wait()
    rows_1 = normalise(1, sums_1)
    for copy in rows_0 + rows_1:
        copy.wait_recv()
    every = jnp.concatenate(
        [unfold(normed[q, j]) for j in range(n_mlp) for q in range(2)], axis=0
    ).astype(BF16)
    acts = []
    for c in range(0, hidden, 2 * LANES):
        end = min(c + 2 * LANES, hidden)
        gate = jnp.dot(every, w_gate[:, c:end], preferred_element_type=F32)
        up = jnp.dot(every, w_up[:, c:end], preferred_element_type=F32)
        acts.append((jax.nn.gelu(gate, approximate=True) * up).astype(BF16))
    act = jnp.concatenate(acts, axis=1)
    span = width // chunks
    last = []
    for c in range(chunks):
        down = jnp.dot(act, w_down[:, c * span : (c + 1) * span], preferred_element_type=F32)
        for j in range(n_mlp):
            part = down[j * rows : (j + 1) * rows, :]
            down_own[c, j] = part
            down_send[c, j] = part.astype(BF16)
        last.append(
            send_all(
                lambda t: down_send.at[c, t],
                lambda d: down_recv.at[c, d],
                lambda d: down_send_sem.at[c, d],
                lambda d: down_recv_sem.at[c, d],
            )
        )
    parts = []
    for c in range(chunks):
        part = h1_own[:, c * span : (c + 1) * span] + down_own[c, m]
        for d in range(1, n_mlp):
            last[c][d - 1].wait_recv()
            part = part + down_recv[c, d].astype(F32)
        parts.append(part)
    h2 = jnp.concatenate(parts, axis=1)
    rf[...] = h2
    for i in range(2 * samp):
        q, s = divmod(i, samp)
        hidden_ref[0, q, s] = rf[2 * i : 2 * i + 2, :].astype(BF16)
    copy = pltpu.make_async_copy(hidden_ref, hidden_hbm, store_sem.at[2])
    copy.start()
    stores.append(copy)
    scale = lax.rsqrt(jnp.mean(h2 * h2, axis=-1, keepdims=True) + 1e-06)
    gain = (norm_final_ref[...] * w_score_ref[...]).reshape(1, width)
    sums = jnp.sum(h2 * scale * gain, axis=-1, keepdims=True)
    col = lax.broadcasted_iota(jnp.int32, (half, samp), 1)
    line = lax.broadcasted_iota(jnp.int32, (half, samp), 0)
    for q in range(2):
        for t in range(2):
            picked = jnp.where(line == 2 * col + t, sums[q * half : (q + 1) * half, :], 0.0)
            scores_ref[0, q, t : t + 1, :] = jnp.sum(picked, axis=0, keepdims=True)
    copy = pltpu.make_async_copy(scores_ref, scores_hbm, store_sem.at[3])
    copy.start()
    stores.append(copy)
    for group in [pages, heads_0, sums_0, rows_0, heads_1, sums_1, rows_1] + last:
        for copy in group:
            copy.wait_send()
    for copy in stores:
        copy.wait()


def hand_over(*refs):
    count = (len(refs) - 1) // 2
    sem = refs[-1]
    copies = [pltpu.make_async_copy(refs[i], refs[count + i], sem.at[i]) for i in range(count)]
    for copy in copies:
        copy.start()
    for copy in copies:
        copy.wait()


def on_device(
    n_req,
    n_mlp,
    queries,
    new_kv,
    residual,
    prompt_kv,
    tail_kv,
    page_pool,
    page_holder,
    serve_slot,
    prompt_len,
    tail_len,
    w_out,
    norm_mlp,
    w_gate,
    w_up,
    w_down,
    norm_final,
    w_score,
):
    samp = queries.shape[2]
    width = residual.shape[-1]
    kv_width = new_kv.shape[-1]
    win = prompt_kv.shape[1]
    tail_rows = tail_kv.shape[2]
    fetched_rows = win + samp * tail_rows
    page = page_pool.shape[1]
    rows = 4 * samp
    block = w_out.shape[0]
    hidden = w_gate.shape[1]
    exchange = page % 16 == 0
    if exchange:
        pool = page_pool
        page_bufs = (n_req, page, kv_width)
    else:
        outgoing = jnp.take(page_pool, serve_slot[0], axis=0)
        arrived = lax.all_to_all(outgoing, "req", split_axis=0, concat_axis=0, tiled=True)
        pool = jnp.take(arrived, page_holder[0], axis=0).reshape(-1, kv_width)
        page_bufs = (1, 16, kv_width)
    pool_buf = page_pool.shape if exchange else page_bufs
    hbm = pl.BlockSpec(memory_space=pltpu.HBM)
    sems = n_req if exchange else 1
    chunks = 3
    made = pl.pallas_call(
        functools.partial(block_kernel, n_req, n_mlp, exchange),
        out_shape=(
            jax.ShapeDtypeStruct((1, 2, 2, samp), F32),
            jax.ShapeDtypeStruct(residual.shape, BF16),
            jax.ShapeDtypeStruct((1, 2, samp, tail_rows, kv_width), BF16),
        ),
        in_specs=[hbm] * 17,
        out_specs=(hbm, hbm, hbm),
        scratch_shapes=[
            pltpu.VMEM((1, 2, 2, samp), F32),
            pltpu.VMEM(residual.shape, BF16),
            pltpu.VMEM((1, 2, samp, tail_rows, kv_width), BF16),
            pltpu.SMEM(page_holder.shape, jnp.int32),
            pltpu.SMEM(serve_slot.shape, jnp.int32),
            pltpu.SMEM(prompt_len.shape, jnp.int32),
            pltpu.SMEM(tail_len.shape, jnp.int32),
            pltpu.VMEM(queries.shape, BF16),
            pltpu.VMEM(new_kv.shape, BF16),
            pltpu.VMEM(residual.shape, BF16),
            pltpu.VMEM(norm_mlp.shape, F32),
            pltpu.VMEM(norm_final.shape, F32),
            pltpu.VMEM(w_score.shape, F32),
            pltpu.VMEM(pool_buf, BF16),
            pltpu.VMEM(page_bufs, BF16),
            pltpu.VMEM(page_bufs, BF16),
            pltpu.VMEM((2, fetched_rows + LANES, kv_width), BF16),
            pltpu.VMEM(w_out.shape, BF16),
            pltpu.VMEM(w_gate.shape, BF16),
            pltpu.VMEM(w_up.shape, BF16),
            pltpu.VMEM(w_down.shape, BF16),
            pltpu.VMEM((rows, queries.shape[-1]), F32),
            pltpu.VMEM((rows, kv_width), F32),
            pltpu.VMEM((rows, width), F32),
            pltpu.VMEM((2, n_mlp, rows // 2, block), F32),
            pltpu.VMEM((2, n_mlp, rows // 2, block), F32),
            pltpu.VMEM((2, n_mlp, rows // 2, width), F32),
            pltpu.VMEM((2, n_mlp, rows, width // 2), BF16),
            pltpu.VMEM((2, n_mlp, rows, width // 2), BF16),
            pltpu.VMEM((2, n_mlp, rows, width // 2), BF16),
            pltpu.VMEM((chunks, n_mlp, rows, width // chunks), F32),
            pltpu.VMEM((chunks, n_mlp, rows, width // chunks), BF16),
            pltpu.VMEM((chunks, n_mlp, rows, width // chunks), BF16),
            pltpu.VMEM((rows, width), F32),
            pltpu.SemaphoreType.DMA((17,)),
            pltpu.SemaphoreType.DMA((sems,)),
            pltpu.SemaphoreType.DMA((sems,)),
            pltpu.SemaphoreType.DMA((3, 2, n_mlp)),
            pltpu.SemaphoreType.DMA((3, 2, n_mlp)),
            pltpu.SemaphoreType.DMA((chunks, n_mlp)),
            pltpu.SemaphoreType.DMA((chunks, n_mlp)),
            pltpu.SemaphoreType.DMA((4,)),
        ],
        compiler_params=pltpu.CompilerParams(
            collective_id=0, has_side_effects=True, vmem_limit_bytes=60 * 1024 * 1024
        ),
        cost_estimate=pl.CostEstimate(
            flops=2 * n_mlp * rows * width * (block + 3 * hidden),
            bytes_accessed=2 * width * (block + 3 * hidden),
            transcendentals=0,
        ),
    )(
        page_holder,
        serve_slot,
        prompt_len,
        tail_len,
        queries,
        new_kv,
        residual,
        norm_mlp,
        norm_final,
        w_score,
        pool,
        prompt_kv.reshape(win, kv_width),
        tail_kv.reshape(samp * tail_rows, kv_width),
        w_out,
        w_gate,
        w_up,
        w_down,
    )
    scores, hidden_out, tails_out = pl.pallas_call(
        hand_over,
        out_shape=tuple(jax.ShapeDtypeStruct(x.shape, x.dtype) for x in made),
        in_specs=[hbm] * 3,
        out_specs=(hbm,) * 3,
        scratch_shapes=[pltpu.SemaphoreType.DMA((3,))],
        compiler_params=pltpu.CompilerParams(vmem_limit_bytes=60 * 1024 * 1024),
    )(*made)
    return jnp.swapaxes(scores, 2, 3), hidden_out, tails_out


def solution(mesh):
    placed = (
        P("req", None, "mlp", None, None),
        P("req", None, "mlp", None, None),
        P("req", None, "mlp", None, None),
        P("req", None, None),
        P("req", "mlp", None, None),
        P(("req", "mlp"), None, None),
        P(("req", "mlp"), None),
        P(("req", "mlp"), None),
        P("req", None),
        P("req", None, "mlp"),
        P("mlp", None),
        P(),
        P(None, "mlp"),
        P(None, "mlp"),
        P("mlp", None),
        P(),
        P(),
    )
    return jax.shard_map(
        functools.partial(on_device, mesh.shape["req"], mesh.shape["mlp"]),
        mesh=mesh,
        in_specs=placed,
        out_specs=(
            P("req", None, "mlp", None),
            P("req", None, "mlp", None, None),
            P("req", None, "mlp", None, None),
        ),
        check_vma=False,
    )
```

```python
import functools

import jax
import jax.numpy as jnp
from jax import lax
from jax.experimental import pallas as pl
from jax.experimental.pallas import tpu as pltpu
from jax.sharding import PartitionSpec as P

F32 = jnp.float32
BF16 = jnp.bfloat16
MESH = pl.DeviceIdType.MESH
HEAD = 128
LANES = 128


def page_order(count):
    half = count // 2
    return sorted(range(1, count), key=lambda d: (abs(d - half), d))


def block_kernel(
    n_req,
    n_mlp,
    exchange,
    holder_hbm,
    slot_hbm,
    plen_hbm,
    tlen_hbm,
    q_hbm,
    new_hbm,
    res_hbm,
    norm_mlp_hbm,
    norm_final_hbm,
    w_score_hbm,
    pool_hbm,
    prompt_hbm,
    tail_hbm,
    w_out_hbm,
    w_gate_hbm,
    w_up_hbm,
    w_down_hbm,
    scores_hbm,
    hidden_hbm,
    tails_hbm,
    scores_ref,
    hidden_ref,
    tails_ref,
    holder_ref,
    slot_ref,
    plen_ref,
    tlen_ref,
    q_ref,
    new_ref,
    res_ref,
    norm_mlp_ref,
    norm_final_ref,
    w_score_ref,
    pool,
    outgoing,
    arrived,
    kv,
    w_out,
    w_gate,
    w_up,
    w_down,
    qf,
    nf,
    rf,
    attn_send,
    attn_recv,
    mix_own,
    mix_send,
    mix_recv,
    normed,
    down_own,
    down_send,
    down_recv,
    h1_own,
    load_sem,
    page_send_sem,
    page_recv_sem,
    mlp_send_sem,
    mlp_recv_sem,
    down_send_sem,
    down_recv_sem,
    store_sem,
):
    samp = q_ref.shape[2]
    width = res_ref.shape[-1]
    rows = 2 * samp * 2
    half = samp * 2
    win = prompt_hbm.shape[0]
    tail_rows = tails_ref.shape[3]
    fetched_rows = win + samp * tail_rows
    kv_rows = kv.shape[1]
    heads = q_ref.shape[-1] // HEAD
    block = w_out_hbm.shape[0]
    hidden = w_gate_hbm.shape[1]
    cut = width // 2
    chunks = down_send.shape[0]
    r = lax.axis_index("req")
    m = lax.axis_index("mlp")

    barrier = pltpu.get_barrier_semaphore()
    peers = n_mlp - 1
    for d in range(1, n_mlp):
        pl.semaphore_signal(
            barrier, inc=1, device_id={"mlp": lax.rem(m + d, n_mlp)}, device_id_type=MESH
        )
    if exchange:
        peers += n_req - 1
        for d in range(1, n_req):
            pl.semaphore_signal(
                barrier, inc=1, device_id={"req": lax.rem(r + d, n_req)}, device_id_type=MESH
            )

    loads = []

    def load(src, dst):
        copy = pltpu.make_async_copy(src, dst, load_sem.at[len(loads)])
        copy.start()
        loads.append(copy)
        return copy

    slot_load = load(slot_hbm, slot_ref)
    pool_load = load(pool_hbm, pool) if exchange else load(pool_hbm, kv.at[1, 0:fetched_rows])
    small = [
        load(holder_hbm, holder_ref),
        load(plen_hbm, plen_ref),
        load(tlen_hbm, tlen_ref),
        load(q_hbm, q_ref),
        load(new_hbm, new_ref),
        load(res_hbm, res_ref),
        load(norm_mlp_hbm, norm_mlp_ref),
        load(norm_final_hbm, norm_final_ref),
        load(w_score_hbm, w_score_ref),
        load(prompt_hbm, kv.at[0, 0:win]),
        load(tail_hbm, kv.at[0, win:fetched_rows]),
    ]
    w_out_load = load(w_out_hbm, w_out)
    w_gate_load = load(w_gate_hbm, w_gate)
    w_up_load = load(w_up_hbm, w_up)
    w_down_load = load(w_down_hbm, w_down)

    pages = []
    slot_load.wait()
    if exchange:
        page = pool.shape[1]
        pool_load.wait()
        for d in page_order(n_req):
            target = lax.rem(r + d, n_req)
            outgoing[target] = pool[slot_ref[0, target]]
        pl.semaphore_wait(barrier, peers)
        for d in page_order(n_req):
            target = lax.rem(r + d, n_req)
            copy = pltpu.make_async_remote_copy(
                src_ref=outgoing.at[target],
                dst_ref=arrived.at[r],
                send_sem=page_send_sem.at[d],
                recv_sem=page_recv_sem.at[d],
                device_id={"req": target},
                device_id_type=MESH,
            )
            copy.start()
            pages.append(copy)
        arrived[r] = pool[slot_ref[0, r]]
    else:
        pl.semaphore_wait(barrier, peers)

    for copy in small:
        copy.wait()
    for i in range(2 * samp):
        q, s = divmod(i, samp)
        qf[2 * i : 2 * i + 2, :] = q_ref[0, q, s].astype(F32)
        nf[2 * i : 2 * i + 2, :] = new_ref[0, q, s].astype(F32)
        rf[2 * i : 2 * i + 2, :] = res_ref[0, q, s].astype(F32)
    fresh = jnp.concatenate(
        [nf[...], jnp.zeros((kv_rows - fetched_rows - rows, nf.shape[1]), F32)], axis=0
    ).astype(BF16)
    kv[0, fetched_rows:kv_rows, :] = fresh
    kv[1, fetched_rows:kv_rows, :] = fresh

    def attend(q):
        own = qf[q * half : (q + 1) * half, :]
        query = jnp.concatenate(
            [own[:, h * HEAD : (h + 1) * HEAD] for h in range(heads)], axis=0
        ).astype(BF16)
        count = heads * half
        scores = lax.dot_general(
            query,
            kv[q, :, 0:HEAD],
            (((1,), (1,)), ((), ())),
            preferred_element_type=F32,
        ) * (1.0 / jnp.sqrt(F32(HEAD)))
        line = lax.broadcasted_iota(jnp.int32, (count, 1), 0) % half
        token = line % 2
        sample = line // 2
        length = jnp.zeros((count, 1), jnp.int32)
        for s in range(samp):
            length = jnp.where(sample == s, tlen_ref[0, q, s], length)
        first = jnp.maximum(win - plen_ref[0, q], length + token + 1)
        col = lax.broadcasted_iota(jnp.int32, (1, win), 1)
        s_win = jnp.where(col >= first, scores[:, 0:win], -1e30)
        col = lax.broadcasted_iota(jnp.int32, (1, samp * tail_rows), 1)
        place = col - sample * tail_rows
        s_tail = jnp.where(
            (place >= 0) & (place < length), scores[:, win:fetched_rows], -1e30
        )
        col = lax.broadcasted_iota(jnp.int32, (1, kv_rows - fetched_rows), 1)
        place = col - (q * half + sample * 2)
        s_new = jnp.where(
            (place >= 0) & (place <= token), scores[:, fetched_rows:kv_rows], -1e30
        )
        scores = jnp.concatenate([s_win, s_tail, s_new], axis=1)
        top = jnp.max(scores, axis=1, keepdims=True)
        e = jnp.exp(scores - top)
        total = jnp.sum(e, axis=1, keepdims=True)
        out = jnp.dot(e.astype(BF16), kv[q, :, HEAD : 2 * HEAD], preferred_element_type=F32)
        return out / total

    def write_tails(q):
        line = lax.broadcasted_iota(jnp.int32, (tail_rows, 1), 0)
        for s in range(samp):
            i = (q * samp + s) * 2
            lead = tlen_ref[0, q, s]
            old = kv[q, win + s * tail_rows : win + (s + 1) * tail_rows, :].astype(F32)
            out = jnp.where(line == lead, nf[i : i + 1, :], old)
            out = jnp.where(line == lead + 1, nf[i + 1 : i + 2, :], out)
            tails_ref[0, q, s] = out.astype(BF16)
        copy = pltpu.make_async_copy(tails_ref.at[0, q], tails_hbm.at[0, q], store_sem.at[q])
        copy.start()
        return copy

    def send_all(source, place, send_sem, recv_sem):
        copies = []
        for d in range(1, n_mlp):
            target = lax.rem(m + d, n_mlp)
            copy = pltpu.make_async_remote_copy(
                src_ref=source(target),
                dst_ref=place(d),
                send_sem=send_sem(d),
                recv_sem=recv_sem(d),
                device_id={"mlp": target},
                device_id_type=MESH,
            )
            copy.start()
            copies.append(copy)
        return copies

    def send_phase(phase, q, source, place):
        return send_all(
            source,
            place,
            lambda d: mlp_send_sem.at[phase, q, d],
            lambda d: mlp_recv_sem.at[phase, q, d],
        )

    def fold(x):
        return jnp.concatenate([x[:, :cut], x[:, cut:]], axis=0).astype(BF16)

    def unfold(x):
        x = x.astype(F32)
        return jnp.concatenate([x[:half], x[half:]], axis=1)

    per = block // HEAD

    def send_heads(q, out):
        for j in range(n_mlp):
            attn_send[q, j] = jnp.concatenate(
                [out[(j * per + h) * half : (j * per + h + 1) * half, :] for h in range(per)],
                axis=1,
            )
        copies = send_phase(
            0, q, lambda t: attn_send.at[q, t], lambda d: attn_recv.at[q, m]
        )
        attn_recv[q, m] = attn_send[q, m]
        return copies

    def project(q, copies):
        for copy in copies:
            copy.wait_recv()
        every = jnp.concatenate([attn_recv[q, j] for j in range(n_mlp)], axis=0).astype(BF16)
        mixed = jnp.dot(every, w_out[...], preferred_element_type=F32)
        for j in range(n_mlp):
            part = mixed[j * half : (j + 1) * half, :]
            mix_own[q, j] = part
            mix_send[q, j] = fold(part)
        return send_phase(1, q, lambda t: mix_send.at[q, t], lambda d: mix_recv.at[q, d])

    def normalise(q, copies):
        total = rf[q * half : (q + 1) * half, :] + mix_own[q, m]
        for copy in copies:
            copy.wait_recv()
        for d in range(1, n_mlp):
            total = total + unfold(mix_recv[q, d])
        h1 = total.astype(BF16).astype(F32)
        h1_own[q * half : (q + 1) * half, :] = h1
        scale = lax.rsqrt(jnp.mean(h1 * h1, axis=-1, keepdims=True) + 1e-06)
        normed[q, m] = fold(h1 * scale * norm_mlp_ref[...].reshape(1, width))
        return send_phase(2, q, lambda t: normed.at[q, m], lambda d: normed.at[q, m])

    done = []
    heads_0 = send_heads(0, attend(0))
    stores = [write_tails(0)]
    w_out_load.wait()
    sums_0 = project(0, heads_0)
    rows_0 = normalise(0, sums_0)

    if exchange:
        for copy in pages:
            copy.wait_recv()
        for p in range(n_req):
            kv[1, p * page : (p + 1) * page, :] = arrived[holder_ref[0, p]]
    else:
        pool_load.wait()
    heads_1 = send_heads(1, attend(1))
    stores.append(write_tails(1))
    sums_1 = project(1, heads_1)
    w_gate_load.wait()
    w_up_load.wait()
    w_down_load.wait()
    rows_1 = normalise(1, sums_1)
    for copy in rows_0 + rows_1:
        copy.wait_recv()
    every = jnp.concatenate(
        [unfold(normed[q, j]) for j in range(n_mlp) for q in range(2)], axis=0
    ).astype(BF16)
    acts = []
    for c in range(0, hidden, 2 * LANES):
        end = min(c + 2 * LANES, hidden)
        gate = jnp.dot(every, w_gate[:, c:end], preferred_element_type=F32)
        up = jnp.dot(every, w_up[:, c:end], preferred_element_type=F32)
        acts.append((jax.nn.gelu(gate, approximate=True) * up).astype(BF16))
    act = jnp.concatenate(acts, axis=1)
    span = width // chunks
    last = []
    for c in range(chunks):
        down = jnp.dot(act, w_down[:, c * span : (c + 1) * span], preferred_element_type=F32)
        for j in range(n_mlp):
            part = down[j * rows : (j + 1) * rows, :]
            down_own[c, j] = part
            down_send[c, j] = part.astype(BF16)
        last.append(
            send_all(
                lambda t: down_send.at[c, t],
                lambda d: down_recv.at[c, d],
                lambda d: down_send_sem.at[c, d],
                lambda d: down_recv_sem.at[c, d],
            )
        )
    parts = []
    for c in range(chunks):
        part = h1_own[:, c * span : (c + 1) * span] + down_own[c, m]
        for d in range(1, n_mlp):
            last[c][d - 1].wait_recv()
            part = part + down_recv[c, d].astype(F32)
        parts.append(part)
    h2 = jnp.concatenate(parts, axis=1)
    rf[...] = h2
    for i in range(2 * samp):
        q, s = divmod(i, samp)
        hidden_ref[0, q, s] = rf[2 * i : 2 * i + 2, :].astype(BF16)
    copy = pltpu.make_async_copy(hidden_ref, hidden_hbm, store_sem.at[2])
    copy.start()
    stores.append(copy)
    scale = lax.rsqrt(jnp.mean(h2 * h2, axis=-1, keepdims=True) + 1e-06)
    gain = (norm_final_ref[...] * w_score_ref[...]).reshape(1, width)
    sums = jnp.sum(h2 * scale * gain, axis=-1, keepdims=True)
    col = lax.broadcasted_iota(jnp.int32, (half, samp), 1)
    line = lax.broadcasted_iota(jnp.int32, (half, samp), 0)
    for q in range(2):
        for t in range(2):
            picked = jnp.where(line == 2 * col + t, sums[q * half : (q + 1) * half, :], 0.0)
            scores_ref[0, q, t : t + 1, :] = jnp.sum(picked, axis=0, keepdims=True)
    copy = pltpu.make_async_copy(scores_ref, scores_hbm, store_sem.at[3])
    copy.start()
    stores.append(copy)
    for group in [pages, heads_0, sums_0, rows_0, heads_1, sums_1, rows_1] + last:
        for copy in group:
            copy.wait_send()
    for copy in stores:
        copy.wait()


def hand_over(*refs):
    count = (len(refs) - 2) // 3
    made, out, held = refs[:count], refs[count : 2 * count], refs[2 * count : 3 * count]
    in_sem, out_sem = refs[-2], refs[-1]
    ins = [pltpu.make_async_copy(made[i], held[i], in_sem.at[i]) for i in range(count)]
    outs = [pltpu.make_async_copy(held[i], out[i], out_sem.at[i]) for i in range(count)]
    for copy in ins:
        copy.start()
    for i in range(count):
        ins[i].wait()
        outs[i].start()
    for copy in outs:
        copy.wait()


def on_device(
    n_req,
    n_mlp,
    queries,
    new_kv,
    residual,
    prompt_kv,
    tail_kv,
    page_pool,
    page_holder,
    serve_slot,
    prompt_len,
    tail_len,
    w_out,
    norm_mlp,
    w_gate,
    w_up,
    w_down,
    norm_final,
    w_score,
):
    samp = queries.shape[2]
    width = residual.shape[-1]
    kv_width = new_kv.shape[-1]
    win = prompt_kv.shape[1]
    tail_rows = tail_kv.shape[2]
    fetched_rows = win + samp * tail_rows
    page = page_pool.shape[1]
    rows = 4 * samp
    block = w_out.shape[0]
    hidden = w_gate.shape[1]
    exchange = page % 16 == 0
    if exchange:
        pool = page_pool
        page_bufs = (n_req, page, kv_width)
    else:
        outgoing = jnp.take(page_pool, serve_slot[0], axis=0)
        arrived = lax.all_to_all(outgoing, "req", split_axis=0, concat_axis=0, tiled=True)
        pool = jnp.take(arrived, page_holder[0], axis=0).reshape(-1, kv_width)
        page_bufs = (1, 16, kv_width)
    pool_buf = page_pool.shape if exchange else page_bufs
    hbm = pl.BlockSpec(memory_space=pltpu.HBM)
    sems = n_req if exchange else 1
    chunks = 3
    made = pl.pallas_call(
        functools.partial(block_kernel, n_req, n_mlp, exchange),
        out_shape=(
            jax.ShapeDtypeStruct((1, 2, 2, samp), F32),
            jax.ShapeDtypeStruct(residual.shape, BF16),
            jax.ShapeDtypeStruct((1, 2, samp, tail_rows, kv_width), BF16),
        ),
        in_specs=[hbm] * 17,
        out_specs=(hbm, hbm, hbm),
        scratch_shapes=[
            pltpu.VMEM((1, 2, 2, samp), F32),
            pltpu.VMEM(residual.shape, BF16),
            pltpu.VMEM((1, 2, samp, tail_rows, kv_width), BF16),
            pltpu.SMEM(page_holder.shape, jnp.int32),
            pltpu.SMEM(serve_slot.shape, jnp.int32),
            pltpu.SMEM(prompt_len.shape, jnp.int32),
            pltpu.SMEM(tail_len.shape, jnp.int32),
            pltpu.VMEM(queries.shape, BF16),
            pltpu.VMEM(new_kv.shape, BF16),
            pltpu.VMEM(residual.shape, BF16),
            pltpu.VMEM(norm_mlp.shape, F32),
            pltpu.VMEM(norm_final.shape, F32),
            pltpu.VMEM(w_score.shape, F32),
            pltpu.VMEM(pool_buf, BF16),
            pltpu.VMEM(page_bufs, BF16),
            pltpu.VMEM(page_bufs, BF16),
            pltpu.VMEM((2, fetched_rows + LANES, kv_width), BF16),
            pltpu.VMEM(w_out.shape, BF16),
            pltpu.VMEM(w_gate.shape, BF16),
            pltpu.VMEM(w_up.shape, BF16),
            pltpu.VMEM(w_down.shape, BF16),
            pltpu.VMEM((rows, queries.shape[-1]), F32),
            pltpu.VMEM((rows, kv_width), F32),
            pltpu.VMEM((rows, width), F32),
            pltpu.VMEM((2, n_mlp, rows // 2, block), F32),
            pltpu.VMEM((2, n_mlp, rows // 2, block), F32),
            pltpu.VMEM((2, n_mlp, rows // 2, width), F32),
            pltpu.VMEM((2, n_mlp, rows, width // 2), BF16),
            pltpu.VMEM((2, n_mlp, rows, width // 2), BF16),
            pltpu.VMEM((2, n_mlp, rows, width // 2), BF16),
            pltpu.VMEM((chunks, n_mlp, rows, width // chunks), F32),
            pltpu.VMEM((chunks, n_mlp, rows, width // chunks), BF16),
            pltpu.VMEM((chunks, n_mlp, rows, width // chunks), BF16),
            pltpu.VMEM((rows, width), F32),
            pltpu.SemaphoreType.DMA((17,)),
            pltpu.SemaphoreType.DMA((sems,)),
            pltpu.SemaphoreType.DMA((sems,)),
            pltpu.SemaphoreType.DMA((3, 2, n_mlp)),
            pltpu.SemaphoreType.DMA((3, 2, n_mlp)),
            pltpu.SemaphoreType.DMA((chunks, n_mlp)),
            pltpu.SemaphoreType.DMA((chunks, n_mlp)),
            pltpu.SemaphoreType.DMA((4,)),
        ],
        compiler_params=pltpu.CompilerParams(
            collective_id=0, has_side_effects=True, vmem_limit_bytes=60 * 1024 * 1024
        ),
        cost_estimate=pl.CostEstimate(
            flops=2 * n_mlp * rows * width * (block + 3 * hidden),
            bytes_accessed=2 * width * (block + 3 * hidden),
            transcendentals=0,
        ),
    )(
        page_holder,
        serve_slot,
        prompt_len,
        tail_len,
        queries,
        new_kv,
        residual,
        norm_mlp,
        norm_final,
        w_score,
        pool,
        prompt_kv.reshape(win, kv_width),
        tail_kv.reshape(samp * tail_rows, kv_width),
        w_out,
        w_gate,
        w_up,
        w_down,
    )
    scores, hidden_out, tails_out = pl.pallas_call(
        hand_over,
        out_shape=tuple(jax.ShapeDtypeStruct(x.shape, x.dtype) for x in made),
        in_specs=[hbm] * 3,
        out_specs=(hbm,) * 3,
        scratch_shapes=[pltpu.VMEM(x.shape, x.dtype) for x in made]
        + [pltpu.SemaphoreType.DMA((3,)), pltpu.SemaphoreType.DMA((3,))],
        compiler_params=pltpu.CompilerParams(vmem_limit_bytes=60 * 1024 * 1024),
    )(*made)
    return jnp.swapaxes(scores, 2, 3), hidden_out, tails_out


def solution(mesh):
    placed = (
        P("req", None, "mlp", None, None),
        P("req", None, "mlp", None, None),
        P("req", None, "mlp", None, None),
        P("req", None, None),
        P("req", "mlp", None, None),
        P(("req", "mlp"), None, None),
        P(("req", "mlp"), None),
        P(("req", "mlp"), None),
        P("req", None),
        P("req", None, "mlp"),
        P("mlp", None),
        P(),
        P(None, "mlp"),
        P(None, "mlp"),
        P("mlp", None),
        P(),
        P(),
    )
    return jax.shard_map(
        functools.partial(on_device, mesh.shape["req"], mesh.shape["mlp"]),
        mesh=mesh,
        in_specs=placed,
        out_specs=(
            P("req", None, "mlp", None),
            P("req", None, "mlp", None, None),
            P("req", None, "mlp", None, None),
        ),
        check_vma=False,
    )
```
